32 devices in a mesh: prow: 8 (over y, x, core), pcol: 4 (over z).
Axes of the slice: x: 2, y: 2, z: 4, core: 2. Of those that a mesh axis runs over, the one named last changes fastest.
Arguments:
- right_side: bfloat16 [5, 32, 128, 256], P(None, ('prow', 'pcol')), may hold values from -6 to 6
- lower_inverse: bfloat16 [5, 32, 128, 128], P(None, ('prow', 'pcol')), may hold values from -1.5 to 1.5
- upper_inverse: bfloat16 [5, 32, 128, 128], P(None, ('prow', 'pcol')), may hold values from -1.5 to 1.5
- lower_blocks: bfloat16 [4, 32, 24, 128, 128], P(None, 'prow', 'pcol'), may hold values from -0.078125 to 0.078125
- lower_index: int32 [4, 32, 24], P(None, 'prow', 'pcol'), may hold values from 0 to 31, as said below
- upper_blocks: bfloat16 [4, 32, 24, 128, 128], P(None, 'prow', 'pcol'), may hold values from -0.078125 to 0.078125
- upper_index: int32 [4, 32, 24], P(None, 'prow', 'pcol'), may hold values from 8 to 39, as said below
Outputs:
- solution: bfloat16 [5, 32, 128, 256], P(None, ('prow', 'pcol'))
The draws below stay inside these ranges and needn't reach their ends.
Inputs may be any that keep to these rules, and one draw needn't show every extreme that they name: lower_index[l, m, j] names a supernode of a level below l + 1; numbers may repeat. upper_index[l, m, j] names a supernode of a level above l; numbers may repeat.
All inputs are finite; a program needn't handle non-finite values.
Results may differ from the reference program's by a relative error of at most 0.014.
Values may be sent and summed in bfloat16 or wider, within the bound.
A program may use at most 128 MiB of HBM per device.

```python
import jax
import jax.numpy as jnp
from jax import lax

W = 128
NRHS = 256
NL = 5
NNZ = 6
SUP_DEV = 1
M = 32
N_PROW = 8
N_PCOL = 4


def assemble(offdiag, key):
    diagonal = jax.random.uniform(key, (NL, M, W, 1), jnp.float32, 0.5, 0.8)
    identity = (jnp.arange(W)[:, None] == jnp.arange(W)[None, :]).astype(jnp.float32)
    return (diagonal * identity + 0.4 * W ** (-0.5) * offdiag).astype(jnp.bfloat16)


def draw_lower_inverse(key, part):
    key = jax.random.fold_in(key, 11)
    first, second = jax.random.split(key)
    offdiag = jnp.clip(jax.random.normal(first, (NL, M, W, W), jnp.float32), -4.0, 4.0)
    return assemble(offdiag, second)


def draw_upper_inverse(key, part):
    key = jax.random.fold_in(key, 17)
    first, second = jax.random.split(key)
    offdiag = jnp.clip(jax.random.normal(first, (NL, M, W, W), jnp.float32), -4.0, 4.0)
    return assemble(offdiag, second)


def draw_lower_index(key, part):
    key = jax.random.fold_in(key, 23)
    first, second = jax.random.split(key)
    per_group = N_PROW * SUP_DEV
    shape = (NL - 1, M, N_PCOL * NNZ)
    ceiling = jnp.arange(1, NL, dtype=jnp.int32)[:, None, None]
    height = jax.random.randint(first, shape, 0, ceiling, dtype=jnp.int32)
    entry = jax.random.randint(second, shape, 0, per_group, dtype=jnp.int32)
    pointers = height * per_group + entry
    pointers = pointers.at[0, 0, 0].set(0)
    pointers = pointers.at[NL - 2, 0, N_PCOL * NNZ - 1].set((NL - 1) * per_group - 1)
    return pointers.astype(jnp.int32)


def draw_upper_index(key, part):
    key = jax.random.fold_in(key, 29)
    first, second = jax.random.split(key)
    per_group = N_PROW * SUP_DEV
    shape = (NL - 1, M, N_PCOL * NNZ)
    floor_level = jnp.arange(1, NL, dtype=jnp.int32)[:, None, None]
    height = jax.random.randint(first, shape, floor_level, NL, dtype=jnp.int32)
    entry = jax.random.randint(second, shape, 0, per_group, dtype=jnp.int32)
    pointers = height * per_group + entry
    pointers = pointers.at[0, 0, 0].set(per_group)
    pointers = pointers.at[0, 0, N_PCOL * NNZ - 1].set(NL * per_group - 1)
    return pointers.astype(jnp.int32)


def steps_of(own_key, shape, cuts, smallest, high):
    factor_of, own = 1.0, jax.random.fold_in(own_key, 6)
    for position, shards_of in cuts:
        heights = jnp.exp(jax.random.uniform(jax.random.fold_in(own, position), (shards_of,), jnp.float32, smallest / len(cuts), high / len(cuts)))
        factor_of = factor_of * jnp.repeat(heights, shape[position] // shards_of).reshape([-1 if axis == position else 1 for axis in range(len(shape))])
    return factor_of


def scatter_about(stream_key, shape, deviation, reach, cuts=(), kind=jnp.bfloat16):
    loudness = steps_of(stream_key, shape, cuts, -0.22, 0.18) if cuts else 1.0
    drawn = jax.random.normal(stream_key, shape, jnp.float32) * deviation * loudness
    return jnp.minimum(jnp.maximum(drawn, -reach), reach).astype(kind)


def setup_inputs(seed: int = 0) -> dict:
    splits = jax.random.split(jax.random.key(seed), 8)
    return {
        "right_side": scatter_about(splits[0], (NL, M, W, NRHS), 1.0, 6.0, ((1, 32),)),
        "lower_inverse": draw_lower_inverse(jax.random.fold_in(splits[7], 71), 0),
        "upper_inverse": draw_upper_inverse(jax.random.fold_in(splits[7], 71), 0),
        "lower_blocks": scatter_about(splits[3], (NL - 1, M, N_PCOL * NNZ, W, W), (2 * W * NNZ * N_PCOL) ** -0.5, 0.078125, ((1, 8), (2, 4))),
        "lower_index": draw_lower_index(jax.random.fold_in(splits[7], 71), 0),
        "upper_blocks": scatter_about(splits[5], (NL - 1, M, N_PCOL * NNZ, W, W), (2 * W * NNZ * N_PCOL) ** -0.5, 0.078125, ((1, 8), (2, 4))),
        "upper_index": draw_upper_index(jax.random.fold_in(splits[7], 71), 0),
    }


def node_ids(pointers):
    per_group = N_PROW * SUP_DEV
    height = pointers // per_group
    entry = pointers % per_group
    owner = (jnp.arange(N_PCOL * NNZ, dtype=jnp.int32) // NNZ)[None, :]
    node = ((entry // SUP_DEV) * N_PCOL + owner) * SUP_DEV + entry % SUP_DEV
    return (height * M + node).astype(jnp.int32)


def level_sums(blocks, pointers, stored):
    ids = node_ids(pointers)

    def one_row(item):
        block_row, id_row = item
        picked = jnp.take(stored, id_row, axis=0).astype(jnp.float32)
        return jnp.einsum("kvw,kwn->vn", block_row.astype(jnp.float32), picked)

    return lax.map(one_row, (blocks, ids))


def apply_inverse(inverse, remain):
    product = jnp.einsum("mvw,mwn->mvn", inverse.astype(jnp.float32), remain.astype(jnp.float32))
    return product.astype(jnp.bfloat16)


def reference(right_side, lower_inverse, upper_inverse, lower_blocks, lower_index, upper_blocks, upper_index):
    stored = jnp.zeros((NL * M, W, NRHS), jnp.bfloat16)
    forward = [apply_inverse(lower_inverse[0], right_side[0])]
    for height in range(1, NL):
        stored = stored.at[(height - 1) * M:height * M].set(forward[-1])
        totals = level_sums(lower_blocks[height - 1], lower_index[height - 1], stored)
        remain = (right_side[height].astype(jnp.float32) - totals).astype(jnp.bfloat16)
        forward.append(apply_inverse(lower_inverse[height], remain))
    stored = jnp.zeros((NL * M, W, NRHS), jnp.bfloat16)
    result = [forward[0]] * NL
    result[NL - 1] = apply_inverse(upper_inverse[NL - 1], forward[NL - 1])
    for height in range(NL - 2, -1, -1):
        stored = stored.at[(height + 1) * M:(height + 2) * M].set(result[height + 1])
        totals = level_sums(upper_blocks[height], upper_index[height], stored)
        remain = (forward[height].astype(jnp.float32) - totals).astype(jnp.bfloat16)
        result[height] = apply_inverse(upper_inverse[height], remain)
    return jnp.stack(result)
```

```python
import functools

import jax
import jax.numpy as jnp
from jax import lax
from jax.experimental import pallas as pl
from jax.experimental.pallas import tpu as pltpu
from jax.sharding import PartitionSpec as P

MESH = pl.DeviceIdType.MESH
HALVES = 2


def flip(index, bits):
    bit = 1
    while bit <= bits:
        if bits & bit:
            index = index + bit - 2 * bit * lax.rem(lax.div(index, bit), 2)
        bit *= 2
    return index


def kernel(
    n_row, n_col, levels, nnz,
    rhs, linv, uinv, lblk, ublk, lidx, uidx, out,
    blk, land, cache, psend, precv, own, fsol,
    blk_sem, gather_send, gather_recv, relay_send, part_send, part_recv,
):
    climbs = levels - 1
    turns = 2 * climbs
    width = land.shape[-1]
    row = lax.axis_index("prow")
    col = lax.axis_index("pcol")
    core = lax.rem(row, 2)
    sibling = flip(row, 1)
    planes = [flip(row, 2 * j) for j in range(1, n_row // 2)]
    ends = [flip(col, j) for j in range(n_col - 1, 0, -1)]

    def block_copy(turn):
        source = lblk.at[turn] if turn < climbs else ublk.at[turns - 1 - turn]
        return pltpu.make_async_copy(source, blk.at[turn], blk_sem.at[turn])

    for turn in range(turns):
        block_copy(turn).start()

    barrier = pltpu.get_barrier_semaphore()
    for peer in planes + [sibling]:
        pl.semaphore_signal(barrier, inc=1, device_id=(peer, col), device_id_type=MESH)
    for peer in ends:
        pl.semaphore_signal(barrier, inc=1, device_id=(row, peer), device_id_type=MESH)

    def gather_copy(turn, half, peer):
        return pltpu.make_async_remote_copy(
            src_ref=land.at[turn, half, row],
            dst_ref=land.at[turn, half, row],
            send_sem=gather_send.at[turn, half, peer],
            recv_sem=gather_recv.at[turn, half, row],
            device_id=(peer, col),
            device_id_type=MESH,
        )

    def gather_arrival(turn, half, slot):
        return pltpu.make_async_remote_copy(
            src_ref=land.at[turn, half, slot],
            dst_ref=land.at[turn, half, slot],
            send_sem=gather_send.at[turn, half, slot],
            recv_sem=gather_recv.at[turn, half, slot],
            device_id=(sibling, col),
            device_id_type=MESH,
        )

    def relay_copy(turn, half, slot):
        return pltpu.make_async_remote_copy(
            src_ref=land.at[turn, half, slot],
            dst_ref=land.at[turn, half, slot],
            send_sem=relay_send.at[turn, half, lax.div(slot, 2)],
            recv_sem=gather_recv.at[turn, half, slot],
            device_id=(sibling, col),
            device_id_type=MESH,
        )

    def part_copy(turn, half, peer):
        return pltpu.make_async_remote_copy(
            src_ref=psend.at[turn, half, peer],
            dst_ref=precv.at[turn, half, col],
            send_sem=part_send.at[turn, half, peer],
            recv_sem=part_recv.at[turn, half, col],
            device_id=(row, peer),
            device_id_type=MESH,
        )

    def part_arrival(turn, half, peer):
        return pltpu.make_async_remote_copy(
            src_ref=psend.at[turn, half, peer],
            dst_ref=precv.at[turn, half, peer],
            send_sem=part_send.at[turn, half, peer],
            recv_sem=part_recv.at[turn, half, peer],
            device_id=(row, peer),
            device_id_type=MESH,
        )

    def columns(half):
        return slice(half * width, (half + 1) * width)

    def apply_inverse(inverse, remain):
        return jnp.dot(inverse, remain, preferred_element_type=jnp.float32).astype(jnp.bfloat16)

    def start_gather(turn, half, level, solved):
        land[turn, half, row] = solved
        for peer in planes:
            gather_copy(turn, half, peer).start()
        gather_copy(turn, half, sibling).start()
        cache[half, level * n_row + row] = solved

    def finish_gather(turn, half, level):
        for peer in planes:
            gather_arrival(turn, half, peer).wait_recv()
            relay_copy(turn, half, peer).start()
            cache[half, level * n_row + peer] = land[turn, half, peer]
        for slot in [sibling] + [flip(peer, 1) for peer in planes]:
            gather_arrival(turn, half, slot).wait_recv()
            cache[half, level * n_row + slot] = land[turn, half, slot]

    def finish_gather_sends(turn, half):
        for peer in planes + [sibling]:
            gather_copy(turn, half, peer).wait_send()
        for peer in planes:
            relay_copy(turn, half, peer).wait_send()

    def row_sum(turn, half, index, level, peer):
        left = jnp.concatenate([blk[turn, peer, k] for k in range(nnz)], axis=1)
        right = jnp.concatenate(
            [cache[half, index[level, peer, k]] for k in range(nnz)], axis=0
        )
        return jnp.dot(left, right, preferred_element_type=jnp.float32)

    def send_parts(turn, half, index, level):
        for peer in ends:
            psend[turn, half, peer] = row_sum(turn, half, index, level, peer).astype(jnp.bfloat16)
            part_copy(turn, half, peer).start()
        own[half] = row_sum(turn, half, index, level, col)

    def take_parts(turn, half):
        total = own[half]
        for peer in ends[::-1]:
            part_arrival(turn, half, peer).wait_recv()
            total = total + precv[turn, half, peer].astype(jnp.float32)
        return total

    def finish_part_sends(turn, half):
        for peer in ends:
            part_copy(turn, half, peer).wait_send()

    def step(turn, forward, last):
        before = turn if forward else turns - turn
        height = turn + 1 if forward else turns - 1 - turn
        index, level = (lidx, turn) if forward else (uidx, height)
        pltpu.make_async_copy(lblk.at[0], blk.at[turn], blk_sem.at[turn]).wait()
        for half in range(HALVES):
            finish_gather(turn, half, before)
            send_parts(turn, half, index, level)
        for half in range(HALVES):
            finish_gather_sends(turn, half)
            total = take_parts(turn, half)
            source = rhs[height, 0, :, columns(half)] if forward else fsol[height, half]
            remain = (source.astype(jnp.float32) - total).astype(jnp.bfloat16)
            if forward:
                solved = apply_inverse(linv[height, 0], remain)
                if last:
                    solved = apply_inverse(uinv[height, 0], solved)
                    out[height, 0, :, columns(half)] = solved
                else:
                    fsol[height, half] = solved
            else:
                solved = apply_inverse(uinv[height, 0], remain)
                out[height, 0, :, columns(half)] = solved
            if forward or not last:
                start_gather(turn + 1, half, height, solved)
            finish_part_sends(turn, half)

    first = []
    for half in range(HALVES):
        solved = apply_inverse(linv[0, 0], rhs[0, 0, :, columns(half)])
        fsol[0, half] = solved
        first.append(solved)
    pl.semaphore_wait(barrier, len(planes) + 1 + len(ends))
    for half in range(HALVES):
        start_gather(0, half, 0, first[half])

    lax.fori_loop(0, climbs - 1, lambda turn, _: step(turn, True, False), None)
    step(climbs - 1, True, True)
    lax.fori_loop(climbs, turns - 1, lambda turn, _: step(turn, False, False), None)
    step(turns - 1, False, True)


def shards(
    right_side, lower_inverse, upper_inverse, lower_blocks, lower_index, upper_blocks, upper_index
):
    n_row, n_col = lax.axis_size("prow"), lax.axis_size("pcol")
    levels, _, breadth, columns = right_side.shape
    climbs, rows, nnz = lower_index.shape
    turns = 2 * climbs
    width = columns // HALVES
    bf16 = jnp.bfloat16
    vmem = pl.BlockSpec(memory_space=pltpu.VMEM)
    smem = pl.BlockSpec(memory_space=pltpu.SMEM)
    hbm = pl.BlockSpec(memory_space=pl.ANY)
    dma = pltpu.SemaphoreType.DMA
    return pl.pallas_call(
        functools.partial(kernel, n_row, n_col, levels, nnz),
        out_shape=jax.ShapeDtypeStruct(right_side.shape, bf16),
        in_specs=[vmem, vmem, vmem, hbm, hbm, smem, smem],
        out_specs=vmem,
        scratch_shapes=[
            pltpu.VMEM((turns, rows, nnz, breadth, breadth), bf16),
            pltpu.VMEM((turns, HALVES, n_row, breadth, width), bf16),
            pltpu.VMEM((HALVES, levels * n_row, breadth, width), bf16),
            pltpu.VMEM((turns, HALVES, n_col, breadth, width), bf16),
            pltpu.VMEM((turns, HALVES, n_col, breadth, width), bf16),
            pltpu.VMEM((HALVES, breadth, width), jnp.float32),
            pltpu.VMEM((levels, HALVES, breadth, width), bf16),
            dma((turns,)),
            dma((turns, HALVES, n_row)),
            dma((turns, HALVES, n_row)),
            dma((turns, HALVES, n_row // 2)),
            dma((turns, HALVES, n_col)),
            dma((turns, HALVES, n_col)),
        ],
        compiler_params=pltpu.CompilerParams(
            collective_id=0, has_side_effects=True, vmem_limit_bytes=58 * 1024 * 1024
        ),
        cost_estimate=pl.CostEstimate(
            flops=2 * turns * rows * nnz * breadth * breadth * columns,
            bytes_accessed=2 * turns * rows * nnz * breadth * breadth,
            transcendentals=0,
        ),
    )(
        right_side, lower_inverse, upper_inverse,
        lower_blocks, upper_blocks, lower_index, upper_index,
    )


def solution(mesh):
    placed = (
        P(None, ("prow", "pcol"), None, None),
        P(None, ("prow", "pcol"), None, None),
        P(None, ("prow", "pcol"), None, None),
        P(None, "prow", "pcol", None, None),
        P(None, "prow", "pcol"),
        P(None, "prow", "pcol", None, None),
        P(None, "prow", "pcol"),
    )
    return jax.shard_map(
        shards,
        mesh=mesh,
        in_specs=placed,
        out_specs=P(None, ("prow", "pcol"), None, None),
        check_vma=False,
    )
```

```python
import functools

import jax
import jax.numpy as jnp
from jax import lax
from jax.experimental import pallas as pl
from jax.experimental.pallas import tpu as pltpu
from jax.sharding import PartitionSpec as P

MESH = pl.DeviceIdType.MESH
HALVES = 2


def flip(index, bits):
    bit = 1
    while bit <= bits:
        if bits & bit:
            index = index + bit - 2 * bit * lax.rem(lax.div(index, bit), 2)
        bit *= 2
    return index


def kernel(
    n_row, n_col, levels, nnz,
    rhs_hbm, linv_hbm, uinv_hbm, lblk, ublk, lidx, uidx, out_hbm,
    rhs, linv, uinv, out, blk, land, cache, psend, precv, own, fsol,
    small_sem, out_sem, blk_sem, gather_send, gather_recv, relay_send, part_send, part_recv,
):
    climbs = levels - 1
    turns = 2 * climbs
    width = land.shape[-1]
    row = lax.axis_index("prow")
    col = lax.axis_index("pcol")
    core = lax.rem(row, 2)
    sibling = flip(row, 1)
    strides = range(n_row // 2 - 1, 0, -1)
    far = [flip(row, 2 * j) for j in strides if j & (j - 1)]
    near = [flip(row, 2 * j) for j in strides if not j & (j - 1)]
    cross = [flip(row, 2 * j + 1) for j in strides if not j & (j - 1)]
    relayed = [flip(peer, 1) for peer in far]
    friends = far + [sibling] + near + cross
    ends = [flip(col, j) for j in range(n_col - 1, 0, -1)]

    def block_copy(turn):
        source = lblk.at[turn] if turn < climbs else ublk.at[turns - 1 - turn]
        return pltpu.make_async_copy(source, blk.at[turn], blk_sem.at[turn])

    smalls = [
        pltpu.make_async_copy(source, target, small_sem.at[place])
        for place, (source, target) in enumerate(((linv_hbm, linv), (rhs_hbm, rhs), (uinv_hbm, uinv)))
    ]

    def out_copy(height):
        return pltpu.make_async_copy(out.at[height], out_hbm.at[height], out_sem.at[height])

    barrier = pltpu.get_barrier_semaphore()
    for peer in friends:
        pl.semaphore_signal(barrier, inc=1, device_id=(peer, col), device_id_type=MESH)
    for peer in ends:
        pl.semaphore_signal(barrier, inc=1, device_id=(row, peer), device_id_type=MESH)

    for copy in smalls:
        copy.start()
    for turn in range(turns):
        block_copy(turn).start()

    def gather_copy(turn, half, peer):
        return pltpu.make_async_remote_copy(
            src_ref=land.at[turn, half, row],
            dst_ref=land.at[turn, half, row],
            send_sem=gather_send.at[turn, half, peer],
            recv_sem=gather_recv.at[turn, half, row],
            device_id=(peer, col),
            device_id_type=MESH,
        )

    def gather_arrival(turn, half, slot):
        return pltpu.make_async_remote_copy(
            src_ref=land.at[turn, half, slot],
            dst_ref=land.at[turn, half, slot],
            send_sem=gather_send.at[turn, half, slot],
            recv_sem=gather_recv.at[turn, half, slot],
            device_id=(sibling, col),
            device_id_type=MESH,
        )

    def relay_copy(turn, half, slot):
        return pltpu.make_async_remote_copy(
            src_ref=land.at[turn, half, slot],
            dst_ref=land.at[turn, half, slot],
            send_sem=relay_send.at[turn, half, lax.div(slot, 2)],
            recv_sem=gather_recv.at[turn, half, slot],
            device_id=(sibling, col),
            device_id_type=MESH,
        )

    def part_copy(turn, half, peer):
        return pltpu.make_async_remote_copy(
            src_ref=psend.at[turn, half, peer],
            dst_ref=precv.at[turn, half, col],
            send_sem=part_send.at[turn, half, peer],
            recv_sem=part_recv.at[turn, half, col],
            device_id=(row, peer),
            device_id_type=MESH,
        )

    def part_arrival(turn, half, peer):
        return pltpu.make_async_remote_copy(
            src_ref=psend.at[turn, half, peer],
            dst_ref=precv.at[turn, half, peer],
            send_sem=part_send.at[turn, half, peer],
            recv_sem=part_recv.at[turn, half, peer],
            device_id=(row, peer),
            device_id_type=MESH,
        )

    def columns(half):
        return slice(half * width, (half + 1) * width)

    def apply_inverse(inverse, remain):
        return jnp.dot(inverse, remain, preferred_element_type=jnp.float32).astype(jnp.bfloat16)

    def start_gather(turn, half, level, solved):
        land[turn, half, row] = solved
        for peer in friends:
            gather_copy(turn, half, peer).start()
        cache[half, level * n_row + row] = solved

    def finish_gather(turn, half, level):
        for peer in far:
            gather_arrival(turn, half, peer).wait_recv()
            relay_copy(turn, half, peer).start()
            cache[half, level * n_row + peer] = land[turn, half, peer]
        for slot in [sibling] + near + cross + relayed:
            gather_arrival(turn, half, slot).wait_recv()
            cache[half, level * n_row + slot] = land[turn, half, slot]

    def finish_gather_sends(turn, half):
        for peer in friends:
            gather_copy(turn, half, peer).wait_send()
        for peer in far:
            relay_copy(turn, half, peer).wait_send()

    def row_sum(turn, half, index, level, peer):
        left = jnp.concatenate([blk[turn, peer, k] for k in range(nnz)], axis=1)
        right = jnp.concatenate(
            [cache[half, index[level, peer, k]] for k in range(nnz)], axis=0
        )
        return jnp.dot(left, right, preferred_element_type=jnp.float32)

    def send_parts(turn, half, index, level):
        for peer in ends:
            psend[turn, half, peer] = row_sum(turn, half, index, level, peer).astype(jnp.bfloat16)
            part_copy(turn, half, peer).start()
        own[half] = row_sum(turn, half, index, level, col)

    def take_parts(turn, half):
        total = own[half]
        for peer in ends[::-1]:
            part_arrival(turn, half, peer).wait_recv()
            total = total + precv[turn, half, peer].astype(jnp.float32)
        return total

    def finish_part_sends(turn, half):
        for peer in ends:
            part_copy(turn, half, peer).wait_send()

    def step(turn, forward, last):
        before = turn if forward else turns - turn
        height = turn + 1 if forward else turns - 1 - turn
        index, level = (lidx, turn) if forward else (uidx, height)
        pltpu.make_async_copy(lblk.at[0], blk.at[turn], blk_sem.at[turn]).wait()
        for half in range(HALVES):
            finish_gather(turn, half, before)
            send_parts(turn, half, index, level)
        for half in range(HALVES):
            finish_gather_sends(turn, half)
            total = take_parts(turn, half)
            source = rhs[height, 0, :, columns(half)] if forward else fsol[height, half]
            remain = (source.astype(jnp.float32) - total).astype(jnp.bfloat16)
            if forward:
                solved = apply_inverse(linv[height, 0], remain)
                if last:
                    solved = apply_inverse(uinv[height, 0], solved)
                    out[height, 0, :, columns(half)] = solved
                else:
                    fsol[height, half] = solved
            else:
                solved = apply_inverse(uinv[height, 0], remain)
                out[height, 0, :, columns(half)] = solved
            if forward or not last:
                start_gather(turn + 1, half, height, solved)
            finish_part_sends(turn, half)
        if last or not forward:
            out_copy(height).start()

    first = []
    for copy in smalls:
        copy.wait()
    for half in range(HALVES):
        solved = apply_inverse(linv[0, 0], rhs[0, 0, :, columns(half)])
        fsol[0, half] = solved
        first.append(solved)
    pl.semaphore_wait(barrier, len(friends) + len(ends))
    for half in range(HALVES):
        start_gather(0, half, 0, first[half])

    lax.fori_loop(0, climbs - 1, lambda turn, _: step(turn, True, False), None)
    step(climbs - 1, True, True)
    lax.fori_loop(climbs, turns - 1, lambda turn, _: step(turn, False, False), None)
    step(turns - 1, False, True)
    for height in range(levels):
        out_copy(height).wait()


def shards(
    right_side, lower_inverse, upper_inverse, lower_blocks, lower_index, upper_blocks, upper_index
):
    n_row, n_col = lax.axis_size("prow"), lax.axis_size("pcol")
    levels, _, breadth, columns = right_side.shape
    climbs, rows, nnz = lower_index.shape
    turns = 2 * climbs
    width = columns // HALVES
    bf16 = jnp.bfloat16
    smem = pl.BlockSpec(memory_space=pltpu.SMEM)
    hbm = pl.BlockSpec(memory_space=pl.ANY)
    dma = pltpu.SemaphoreType.DMA
    return pl.pallas_call(
        functools.partial(kernel, n_row, n_col, levels, nnz),
        out_shape=jax.ShapeDtypeStruct(right_side.shape, bf16),
        in_specs=[hbm, hbm, hbm, hbm, hbm, smem, smem],
        out_specs=hbm,
        scratch_shapes=[
            pltpu.VMEM(right_side.shape, bf16),
            pltpu.VMEM(lower_inverse.shape, bf16),
            pltpu.VMEM(upper_inverse.shape, bf16),
            pltpu.VMEM(right_side.shape, bf16),
            pltpu.VMEM((turns, rows, nnz, breadth, breadth), bf16),
            pltpu.VMEM((turns, HALVES, n_row, breadth, width), bf16),
            pltpu.VMEM((HALVES, levels * n_row, breadth, width), bf16),
            pltpu.VMEM((turns, HALVES, n_col, breadth, width), bf16),
            pltpu.VMEM((turns, HALVES, n_col, breadth, width), bf16),
            pltpu.VMEM((HALVES, breadth, width), jnp.float32),
            pltpu.VMEM((levels, HALVES, breadth, width), bf16),
            dma((3,)),
            dma((levels,)),
            dma((turns,)),
            dma((turns, HALVES, n_row)),
            dma((turns, HALVES, n_row)),
            dma((turns, HALVES, n_row // 2)),
            dma((turns, HALVES, n_col)),
            dma((turns, HALVES, n_col)),
        ],
        compiler_params=pltpu.CompilerParams(
            collective_id=0, has_side_effects=True, vmem_limit_bytes=58 * 1024 * 1024
        ),
        cost_estimate=pl.CostEstimate(
            flops=2 * turns * rows * nnz * breadth * breadth * columns,
            bytes_accessed=2 * turns * rows * nnz * breadth * breadth,
            transcendentals=0,
        ),
    )(
        right_side, lower_inverse, upper_inverse,
        lower_blocks, upper_blocks, lower_index, upper_index,
    )


def solution(mesh):
    placed = (
        P(None, ("prow", "pcol"), None, None),
        P(None, ("prow", "pcol"), None, None),
        P(None, ("prow", "pcol"), None, None),
        P(None, "prow", "pcol", None, None),
        P(None, "prow", "pcol"),
        P(None, "prow", "pcol", None, None),
        P(None, "prow", "pcol"),
    )
    return jax.shard_map(
        shards,
        mesh=mesh,
        in_specs=placed,
        out_specs=P(None, ("prow", "pcol"), None, None),
        check_vma=False,
    )
```

```python
import functools

import jax
import jax.numpy as jnp
from jax import lax
from jax.experimental import pallas as pl
from jax.experimental.pallas import tpu as pltpu
from jax.sharding import PartitionSpec as P

MESH = pl.DeviceIdType.MESH
HALVES = 2


def flip(index, bits):
    bit = 1
    while bit <= bits:
        if bits & bit:
            index = index + bit - 2 * bit * lax.rem(lax.div(index, bit), 2)
        bit *= 2
    return index


def kernel(
    n_row, n_col, levels, nnz,
    rhs_hbm, linv_hbm, uinv_hbm, lblk, ublk, lidx, uidx, out_hbm,
    rhs, linv, uinv, out, blk, land, cache, psend, precv, own, held, fsol,
    small_sem, out_sem, blk_sem, gather_send, gather_recv, relay_send, part_send, part_recv,
):
    climbs = levels - 1
    turns = 2 * climbs
    width = land.shape[-1]
    row = lax.axis_index("prow")
    col = lax.axis_index("pcol")
    core = lax.rem(row, 2)
    sibling = flip(row, 1)
    strides = range(n_row // 2 - 1, 0, -1)
    planes = [flip(row, 2 * j) for j in strides]
    relayed = [flip(peer, 1) for peer in planes]
    friends = planes + [sibling]
    folded = n_col == 4
    ends = [flip(col, j) for j in range(n_col)]
    outer = (col == 0) | (col == n_col - 1)
    inner = jnp.logical_not(outer)
    order = (2, 3, 1) if folded else range(n_col - 1, 0, -1)

    def block_copy(turn):
        source = lblk.at[turn] if turn < climbs else ublk.at[turns - 1 - turn]
        return pltpu.make_async_copy(source, blk.at[turn], blk_sem.at[turn])

    smalls = [
        pltpu.make_async_copy(source, target, small_sem.at[place])
        for place, (source, target) in enumerate(((linv_hbm, linv), (rhs_hbm, rhs), (uinv_hbm, uinv)))
    ]

    def out_copy(height):
        return pltpu.make_async_copy(out.at[height], out_hbm.at[height], out_sem.at[height])

    barrier = pltpu.get_barrier_semaphore()
    for peer in friends:
        pl.semaphore_signal(barrier, inc=1, device_id=(peer, col), device_id_type=MESH)
    for peer in ends[1:]:
        pl.semaphore_signal(barrier, inc=1, device_id=(row, peer), device_id_type=MESH)

    for copy in smalls:
        copy.start()
    for turn in range(turns):
        block_copy(turn).start()

    def gather_copy(turn, half, peer):
        return pltpu.make_async_remote_copy(
            src_ref=land.at[turn, half, row],
            dst_ref=land.at[turn, half, row],
            send_sem=gather_send.at[turn, half, peer],
            recv_sem=gather_recv.at[turn, half, row],
            device_id=(peer, col),
            device_id_type=MESH,
        )

    def gather_arrival(turn, half, slot):
        return pltpu.make_async_remote_copy(
            src_ref=land.at[turn, half, slot],
            dst_ref=land.at[turn, half, slot],
            send_sem=gather_send.at[turn, half, slot],
            recv_sem=gather_recv.at[turn, half, slot],
            device_id=(sibling, col),
            device_id_type=MESH,
        )

    def relay_copy(turn, half, slot):
        return pltpu.make_async_remote_copy(
            src_ref=land.at[turn, half, slot],
            dst_ref=land.at[turn, half, slot],
            send_sem=relay_send.at[turn, half, lax.div(slot, 2)],
            recv_sem=gather_recv.at[turn, half, slot],
            device_id=(sibling, col),
            device_id_type=MESH,
        )

    def part_copy(turn, half, j):
        peer = jnp.where(outer, ends[1], ends[2]) if folded and j == 2 else ends[j]
        return pltpu.make_async_remote_copy(
            src_ref=psend.at[turn, half, j],
            dst_ref=precv.at[turn, half, j],
            send_sem=part_send.at[turn, half, j],
            recv_sem=part_recv.at[turn, half, j],
            device_id=(row, peer),
            device_id_type=MESH,
        )

    def columns(half):
        return slice(half * width, (half + 1) * width)

    def apply_inverse(inverse, remain):
        return jnp.dot(inverse, remain, preferred_element_type=jnp.float32).astype(jnp.bfloat16)

    def start_gather(turn, half, level, solved):
        land[turn, half, row] = solved
        for peer in friends:
            gather_copy(turn, half, peer).start()
        cache[half, level * n_row + row] = solved

    def finish_gather(turn, half, level):
        for peer in planes:
            gather_arrival(turn, half, peer).wait_recv()
            relay_copy(turn, half, peer).start()
            cache[half, level * n_row + peer] = land[turn, half, peer]
        for slot in [sibling] + relayed:
            gather_arrival(turn, half, slot).wait_recv()
            cache[half, level * n_row + slot] = land[turn, half, slot]

    def finish_gather_sends(turn, half):
        for peer in friends:
            gather_copy(turn, half, peer).wait_send()
        for peer in planes:
            relay_copy(turn, half, peer).wait_send()

    def row_sum(turn, half, index, level, peer):
        left = jnp.concatenate([blk[turn, peer, k] for k in range(nnz)], axis=1)
        right = jnp.concatenate(
            [cache[half, index[level, peer, k]] for k in range(nnz)], axis=0
        )
        return jnp.dot(left, right, preferred_element_type=jnp.float32)

    def send_parts(turn, half, index, level):
        for j in order:
            value = row_sum(turn, half, index, level, ends[j])
            if folded and j == 3:
                held[half] = value

                @pl.when(outer)
                def _():
                    psend[turn, half, j] = held[half].astype(jnp.bfloat16)
                    part_copy(turn, half, j).start()
            else:
                psend[turn, half, j] = value.astype(jnp.bfloat16)
                part_copy(turn, half, j).start()
        own[half] = row_sum(turn, half, index, level, col)

    def fold_parts(turn, half):
        @pl.when(inner)
        def _():
            part_copy(turn, half, 2).wait_recv()
            value = held[half] + precv[turn, half, 2].astype(jnp.float32)
            psend[turn, half, 3] = value.astype(jnp.bfloat16)
            part_copy(turn, half, 3).start()

    def take_parts(turn, half):
        for j in order[::-1]:
            if folded and j == 2:
                @pl.when(outer)
                def _():
                    part_copy(turn, half, j).wait_recv()
                    own[half] += precv[turn, half, j].astype(jnp.float32)
            else:
                part_copy(turn, half, j).wait_recv()
                own[half] += precv[turn, half, j].astype(jnp.float32)
        return own[half]

    def finish_part_sends(turn, half):
        for j in order:
            part_copy(turn, half, j).wait_send()

    def step(turn, forward, last):
        before = turn if forward else turns - turn
        height = turn + 1 if forward else turns - 1 - turn
        index, level = (lidx, turn) if forward else (uidx, height)
        pltpu.make_async_copy(lblk.at[0], blk.at[turn], blk_sem.at[turn]).wait()
        for half in range(HALVES):
            finish_gather(turn, half, before)
            send_parts(turn, half, index, level)
            if folded:
                fold_parts(turn, half)
        for half in range(HALVES):
            finish_gather_sends(turn, half)
            total = take_parts(turn, half)
            source = rhs[height, 0, :, columns(half)] if forward else fsol[height, half]
            remain = (source.astype(jnp.float32) - total).astype(jnp.bfloat16)
            if forward:
                solved = apply_inverse(linv[height, 0], remain)
                if last:
                    solved = apply_inverse(uinv[height, 0], solved)
                    out[height, 0, :, columns(half)] = solved
                else:
                    fsol[height, half] = solved
            else:
                solved = apply_inverse(uinv[height, 0], remain)
                out[height, 0, :, columns(half)] = solved
            if forward or not last:
                start_gather(turn + 1, half, height, solved)
            finish_part_sends(turn, half)
        if last or not forward:
            out_copy(height).start()

    first = []
    for copy in smalls:
        copy.wait()
    for half in range(HALVES):
        solved = apply_inverse(linv[0, 0], rhs[0, 0, :, columns(half)])
        fsol[0, half] = solved
        first.append(solved)
    pl.semaphore_wait(barrier, len(friends) + n_col - 1)
    for half in range(HALVES):
        start_gather(0, half, 0, first[half])

    lax.fori_loop(0, climbs - 1, lambda turn, _: step(turn, True, False), None)
    step(climbs - 1, True, True)
    lax.fori_loop(climbs, turns - 1, lambda turn, _: step(turn, False, False), None)
    step(turns - 1, False, True)
    for height in range(levels):
        out_copy(height).wait()


def shards(
    right_side, lower_inverse, upper_inverse, lower_blocks, lower_index, upper_blocks, upper_index
):
    n_row, n_col = lax.axis_size("prow"), lax.axis_size("pcol")
    levels, _, breadth, columns = right_side.shape
    climbs, rows, nnz = lower_index.shape
    turns = 2 * climbs
    width = columns // HALVES
    bf16 = jnp.bfloat16
    smem = pl.BlockSpec(memory_space=pltpu.SMEM)
    hbm = pl.BlockSpec(memory_space=pl.ANY)
    dma = pltpu.SemaphoreType.DMA
    return pl.pallas_call(
        functools.partial(kernel, n_row, n_col, levels, nnz),
        out_shape=jax.ShapeDtypeStruct(right_side.shape, bf16),
        in_specs=[hbm, hbm, hbm, hbm, hbm, smem, smem],
        out_specs=hbm,
        scratch_shapes=[
            pltpu.VMEM(right_side.shape, bf16),
            pltpu.VMEM(lower_inverse.shape, bf16),
            pltpu.VMEM(upper_inverse.shape, bf16),
            pltpu.VMEM(right_side.shape, bf16),
            pltpu.VMEM((turns, rows, nnz, breadth, breadth), bf16),
            pltpu.VMEM((turns, HALVES, n_row, breadth, width), bf16),
            pltpu.VMEM((HALVES, levels * n_row, breadth, width), bf16),
            pltpu.VMEM((turns, HALVES, n_col, breadth, width), bf16),
            pltpu.VMEM((turns, HALVES, n_col, breadth, width), bf16),
            pltpu.VMEM((HALVES, breadth, width), jnp.float32),
            pltpu.VMEM((HALVES, breadth, width), jnp.float32),
            pltpu.VMEM((levels, HALVES, breadth, width), bf16),
            dma((3,)),
            dma((levels,)),
            dma((turns,)),
            dma((turns, HALVES, n_row)),
            dma((turns, HALVES, n_row)),
            dma((turns, HALVES, n_row // 2)),
            dma((turns, HALVES, n_col)),
            dma((turns, HALVES, n_col)),
        ],
        compiler_params=pltpu.CompilerParams(
            collective_id=0, has_side_effects=True, vmem_limit_bytes=58 * 1024 * 1024
        ),
        cost_estimate=pl.CostEstimate(
            flops=2 * turns * rows * nnz * breadth * breadth * columns,
            bytes_accessed=2 * turns * rows * nnz * breadth * breadth,
            transcendentals=0,
        ),
    )(
        right_side, lower_inverse, upper_inverse,
        lower_blocks, upper_blocks, lower_index, upper_index,
    )


def solution(mesh):
    placed = (
        P(None, ("prow", "pcol"), None, None),
        P(None, ("prow", "pcol"), None, None),
        P(None, ("prow", "pcol"), None, None),
        P(None, "prow", "pcol", None, None),
        P(None, "prow", "pcol"),
        P(None, "prow", "pcol", None, None),
        P(None, "prow", "pcol"),
    )
    return jax.shard_map(
        shards,
        mesh=mesh,
        in_specs=placed,
        out_specs=P(None, ("prow", "pcol"), None, None),
        check_vma=False,
    )
```

```python
import functools

import jax
import jax.numpy as jnp
from jax import lax
from jax.experimental import pallas as pl
from jax.experimental.pallas import tpu as pltpu
from jax.sharding import PartitionSpec as P

MESH = pl.DeviceIdType.MESH
HALVES = 1


def flip(index, bits):
    bit = 1
    while bit <= bits:
        if bits & bit:
            index = index + bit - 2 * bit * lax.rem(lax.div(index, bit), 2)
        bit *= 2
    return index


def kernel(
    n_row, n_col, levels, nnz,
    rhs_hbm, linv_hbm, uinv_hbm, lblk, ublk, lidx, uidx, out_hbm,
    rhs, linv, uinv, out, blk, land, cache, psend, precv, own, held, fsol,
    small_sem, out_sem, blk_sem, gather_send, gather_recv, relay_send, part_send, part_recv,
):
    climbs = levels - 1
    turns = 2 * climbs
    width = land.shape[-1]
    row = lax.axis_index("prow")
    col = lax.axis_index("pcol")
    core = lax.rem(row, 2)
    sibling = flip(row, 1)
    strides = range(n_row // 2 - 1, 0, -1)
    planes = [flip(row, 2 * j) for j in strides]
    relayed = [flip(peer, 1) for peer in planes]
    friends = planes + [sibling]
    folded = False
    ends = [flip(col, j) for j in range(n_col)]
    outer = (col == 0) | (col == n_col - 1)
    inner = jnp.logical_not(outer)
    order = (2, 3, 1) if folded else range(n_col - 1, 0, -1)

    def block_copy(turn):
        source = lblk.at[turn] if turn < climbs else ublk.at[turns - 1 - turn]
        return pltpu.make_async_copy(source, blk.at[turn], blk_sem.at[turn])

    smalls = [
        pltpu.make_async_copy(source, target, small_sem.at[place])
        for place, (source, target) in enumerate(((linv_hbm, linv), (rhs_hbm, rhs), (uinv_hbm, uinv)))
    ]

    def out_copy(height):
        return pltpu.make_async_copy(out.at[height], out_hbm.at[height], out_sem.at[height])

    barrier = pltpu.get_barrier_semaphore()
    for peer in friends:
        pl.semaphore_signal(barrier, inc=1, device_id=(peer, col), device_id_type=MESH)
    for peer in ends[1:]:
        pl.semaphore_signal(barrier, inc=1, device_id=(row, peer), device_id_type=MESH)

    for copy in smalls:
        copy.start()
    for turn in range(turns):
        block_copy(turn).start()

    def gather_copy(turn, half, peer):
        return pltpu.make_async_remote_copy(
            src_ref=land.at[turn, half, row],
            dst_ref=land.at[turn, half, row],
            send_sem=gather_send.at[turn, half, peer],
            recv_sem=gather_recv.at[turn, half, row],
            device_id=(peer, col),
            device_id_type=MESH,
        )

    def gather_arrival(turn, half, slot):
        return pltpu.make_async_remote_copy(
            src_ref=land.at[turn, half, slot],
            dst_ref=land.at[turn, half, slot],
            send_sem=gather_send.at[turn, half, slot],
            recv_sem=gather_recv.at[turn, half, slot],
            device_id=(sibling, col),
            device_id_type=MESH,
        )

    def relay_copy(turn, half, slot):
        return pltpu.make_async_remote_copy(
            src_ref=land.at[turn, half, slot],
            dst_ref=land.at[turn, half, slot],
            send_sem=relay_send.at[turn, half, lax.div(slot, 2)],
            recv_sem=gather_recv.at[turn, half, slot],
            device_id=(sibling, col),
            device_id_type=MESH,
        )

    def part_copy(turn, half, j):
        peer = jnp.where(outer, ends[1], ends[2]) if folded and j == 2 else ends[j]
        return pltpu.make_async_remote_copy(
            src_ref=psend.at[turn, half, j],
            dst_ref=precv.at[turn, half, j],
            send_sem=part_send.at[turn, half, j],
            recv_sem=part_recv.at[turn, half, j],
            device_id=(row, peer),
            device_id_type=MESH,
        )

    def columns(half):
        return slice(half * width, (half + 1) * width)

    def apply_inverse(inverse, remain):
        return jnp.dot(inverse, remain, preferred_element_type=jnp.float32).astype(jnp.bfloat16)

    def start_gather(turn, half, level, solved):
        land[turn, half, row] = solved
        for peer in friends:
            gather_copy(turn, half, peer).start()
        cache[half, level * n_row + row] = solved

    def finish_gather(turn, half, level):
        for peer in planes:
            gather_arrival(turn, half, peer).wait_recv()
            relay_copy(turn, half, peer).start()
            cache[half, level * n_row + peer] = land[turn, half, peer]
        for slot in [sibling] + relayed:
            gather_arrival(turn, half, slot).wait_recv()
            cache[half, level * n_row + slot] = land[turn, half, slot]

    def finish_gather_sends(turn, half):
        for peer in friends:
            gather_copy(turn, half, peer).wait_send()
        for peer in planes:
            relay_copy(turn, half, peer).wait_send()

    def row_sum(turn, half, index, level, peer):
        left = jnp.concatenate([blk[turn, peer, k] for k in range(nnz)], axis=1)
        right = jnp.concatenate(
            [cache[half, index[level, peer, k]] for k in range(nnz)], axis=0
        )
        return jnp.dot(left, right, preferred_element_type=jnp.float32)

    def send_parts(turn, half, index, level):
        for j in order:
            value = row_sum(turn, half, index, level, ends[j])
            if folded and j == 3:
                held[half] = value

                @pl.when(outer)
                def _():
                    psend[turn, half, j] = held[half].astype(jnp.bfloat16)
                    part_copy(turn, half, j).start()
            else:
                psend[turn, half, j] = value.astype(jnp.bfloat16)
                part_copy(turn, half, j).start()
        own[half] = row_sum(turn, half, index, level, col)

    def fold_parts(turn, half):
        @pl.when(inner)
        def _():
            part_copy(turn, half, 2).wait_recv()
            value = held[half] + precv[turn, half, 2].astype(jnp.float32)
            psend[turn, half, 3] = value.astype(jnp.bfloat16)
            part_copy(turn, half, 3).start()

    def take_parts(turn, half):
        for j in order[::-1]:
            if folded and j == 2:
                @pl.when(outer)
                def _():
                    part_copy(turn, half, j).wait_recv()
                    own[half] += precv[turn, half, j].astype(jnp.float32)
            else:
                part_copy(turn, half, j).wait_recv()
                own[half] += precv[turn, half, j].astype(jnp.float32)
        return own[half]

    def finish_part_sends(turn, half):
        for j in order:
            part_copy(turn, half, j).wait_send()

    def step(turn, forward, last):
        before = turn if forward else turns - turn
        height = turn + 1 if forward else turns - 1 - turn
        index, level = (lidx, turn) if forward else (uidx, height)
        pltpu.make_async_copy(lblk.at[0], blk.at[turn], blk_sem.at[turn]).wait()
        for half in range(HALVES):
            finish_gather(turn, half, before)
            send_parts(turn, half, index, level)
            if folded:
                fold_parts(turn, half)
        for half in range(HALVES):
            finish_gather_sends(turn, half)
            total = take_parts(turn, half)
            source = rhs[height, 0, :, columns(half)] if forward else fsol[height, half]
            remain = (source.astype(jnp.float32) - total).astype(jnp.bfloat16)
            if forward:
                solved = apply_inverse(linv[height, 0], remain)
                if last:
                    solved = apply_inverse(uinv[height, 0], solved)
                    out[height, 0, :, columns(half)] = solved
                else:
                    fsol[height, half] = solved
            else:
                solved = apply_inverse(uinv[height, 0], remain)
                out[height, 0, :, columns(half)] = solved
            if forward or not last:
                start_gather(turn + 1, half, height, solved)
            finish_part_sends(turn, half)
        if last or not forward:
            out_copy(height).start()

    first = []
    for copy in smalls:
        copy.wait()
    for half in range(HALVES):
        solved = apply_inverse(linv[0, 0], rhs[0, 0, :, columns(half)])
        fsol[0, half] = solved
        first.append(solved)
    pl.semaphore_wait(barrier, len(friends) + n_col - 1)
    for half in range(HALVES):
        start_gather(0, half, 0, first[half])

    lax.fori_loop(0, climbs - 1, lambda turn, _: step(turn, True, False), None)
    step(climbs - 1, True, True)
    lax.fori_loop(climbs, turns - 1, lambda turn, _: step(turn, False, False), None)
    step(turns - 1, False, True)
    for height in range(levels):
        out_copy(height).wait()


def shards(
    right_side, lower_inverse, upper_inverse, lower_blocks, lower_index, upper_blocks, upper_index
):
    n_row, n_col = lax.axis_size("prow"), lax.axis_size("pcol")
    levels, _, breadth, columns = right_side.shape
    climbs, rows, nnz = lower_index.shape
    turns = 2 * climbs
    width = columns // HALVES
    bf16 = jnp.bfloat16
    smem = pl.BlockSpec(memory_space=pltpu.SMEM)
    hbm = pl.BlockSpec(memory_space=pl.ANY)
    dma = pltpu.SemaphoreType.DMA
    return pl.pallas_call(
        functools.partial(kernel, n_row, n_col, levels, nnz),
        out_shape=jax.ShapeDtypeStruct(right_side.shape, bf16),
        in_specs=[hbm, hbm, hbm, hbm, hbm, smem, smem],
        out_specs=hbm,
        scratch_shapes=[
            pltpu.VMEM(right_side.shape, bf16),
            pltpu.VMEM(lower_inverse.shape, bf16),
            pltpu.VMEM(upper_inverse.shape, bf16),
            pltpu.VMEM(right_side.shape, bf16),
            pltpu.VMEM((turns, rows, nnz, breadth, breadth), bf16),
            pltpu.VMEM((turns, HALVES, n_row, breadth, width), bf16),
            pltpu.VMEM((HALVES, levels * n_row, breadth, width), bf16),
            pltpu.VMEM((turns, HALVES, n_col, breadth, width), bf16),
            pltpu.VMEM((turns, HALVES, n_col, breadth, width), bf16),
            pltpu.VMEM((HALVES, breadth, width), jnp.float32),
            pltpu.VMEM((HALVES, breadth, width), jnp.float32),
            pltpu.VMEM((levels, HALVES, breadth, width), bf16),
            dma((3,)),
            dma((levels,)),
            dma((turns,)),
            dma((turns, HALVES, n_row)),
            dma((turns, HALVES, n_row)),
            dma((turns, HALVES, n_row // 2)),
            dma((turns, HALVES, n_col)),
            dma((turns, HALVES, n_col)),
        ],
        compiler_params=pltpu.CompilerParams(
            collective_id=0, has_side_effects=True, vmem_limit_bytes=58 * 1024 * 1024
        ),
        cost_estimate=pl.CostEstimate(
            flops=2 * turns * rows * nnz * breadth * breadth * columns,
            bytes_accessed=2 * turns * rows * nnz * breadth * breadth,
            transcendentals=0,
        ),
    )(
        right_side, lower_inverse, upper_inverse,
        lower_blocks, upper_blocks, lower_index, upper_index,
    )


def solution(mesh):
    placed = (
        P(None, ("prow", "pcol"), None, None),
        P(None, ("prow", "pcol"), None, None),
        P(None, ("prow", "pcol"), None, None),
        P(None, "prow", "pcol", None, None),
        P(None, "prow", "pcol"),
        P(None, "prow", "pcol", None, None),
        P(None, "prow", "pcol"),
    )
    return jax.shard_map(
        shards,
        mesh=mesh,
        in_specs=placed,
        out_specs=P(None, ("prow", "pcol"), None, None),
        check_vma=False,
    )
```

```python
import functools

import jax
import jax.numpy as jnp
from jax import lax
from jax.experimental import pallas as pl
from jax.experimental.pallas import tpu as pltpu
from jax.sharding import PartitionSpec as P

MESH = pl.DeviceIdType.MESH
PIECES = 4


def flip(index, bits):
    bit = 1
    while bit <= bits:
        if bits & bit:
            index = index + bit - 2 * bit * lax.rem(lax.div(index, bit), 2)
        bit *= 2
    return index


def pack(piece):
    count = max(1, 128 // piece.shape[1])
    rows = piece.shape[0] // count
    return jnp.concatenate([piece[i * rows:(i + 1) * rows] for i in range(count)], axis=1)


def unpack(packed, width):
    return jnp.concatenate(
        [packed[:, i:i + width] for i in range(0, packed.shape[1], width)], axis=0
    )


def kernel(
    n_row, n_col, levels, nnz,
    rhs_hbm, linv_hbm, uinv_hbm, lblk, ublk, lidx, uidx, out_hbm,
    rhs, linv, uinv, out, blk, land, cache, psend, precv, own, fsol,
    small_sem, out_sem, blk_sem, gather_send, gather_recv, relay_send, part_send, part_recv,
):
    climbs = levels - 1
    turns = 2 * climbs
    width = cache.shape[-1]
    row = lax.axis_index("prow")
    col = lax.axis_index("pcol")
    core = lax.rem(row, 2)
    sibling = flip(row, 1)
    strides = range(n_row // 2 - 1, 0, -1)
    far = [flip(row, 2 * j) for j in strides if j & (j - 1)]
    near = [flip(row, 2 * j) for j in strides if not j & (j - 1)]
    cross = [flip(row, 2 * j + 1) for j in strides if not j & (j - 1)]
    relayed = [flip(peer, 1) for peer in far]
    friends = far + [sibling] + near + cross
    ends = [flip(col, j) for j in range(n_col - 1, 0, -1)]

    def block_copy(turn):
        source = lblk.at[turn] if turn < climbs else ublk.at[turns - 1 - turn]
        return pltpu.make_async_copy(source, blk.at[turn], blk_sem.at[turn])

    smalls = [
        pltpu.make_async_copy(source, target, small_sem.at[place])
        for place, (source, target) in enumerate(((linv_hbm, linv), (rhs_hbm, rhs), (uinv_hbm, uinv)))
    ]

    def out_copy(height):
        return pltpu.make_async_copy(out.at[height], out_hbm.at[height], out_sem.at[height])

    barrier = pltpu.get_barrier_semaphore()
    for peer in friends:
        pl.semaphore_signal(barrier, inc=1, device_id=(peer, col), device_id_type=MESH)
    for peer in ends:
        pl.semaphore_signal(barrier, inc=1, device_id=(row, peer), device_id_type=MESH)

    for copy in smalls:
        copy.start()
    for turn in range(turns):
        block_copy(turn).start()

    def gather_copy(turn, piece, peer):
        return pltpu.make_async_remote_copy(
            src_ref=land.at[turn, piece, row],
            dst_ref=land.at[turn, piece, row],
            send_sem=gather_send.at[turn, piece, peer],
            recv_sem=gather_recv.at[turn, piece, row],
            device_id=(peer, col),
            device_id_type=MESH,
        )

    def gather_arrival(turn, piece, slot):
        return pltpu.make_async_remote_copy(
            src_ref=land.at[turn, piece, slot],
            dst_ref=land.at[turn, piece, slot],
            send_sem=gather_send.at[turn, piece, slot],
            recv_sem=gather_recv.at[turn, piece, slot],
            device_id=(sibling, col),
            device_id_type=MESH,
        )

    def relay_copy(turn, piece, slot):
        return pltpu.make_async_remote_copy(
            src_ref=land.at[turn, piece, slot],
            dst_ref=land.at[turn, piece, slot],
            send_sem=relay_send.at[turn, piece, lax.div(slot, 2)],
            recv_sem=gather_recv.at[turn, piece, slot],
            device_id=(sibling, col),
            device_id_type=MESH,
        )

    def part_copy(turn, piece, peer):
        return pltpu.make_async_remote_copy(
            src_ref=psend.at[turn, piece, peer],
            dst_ref=precv.at[turn, piece, col],
            send_sem=part_send.at[turn, piece, peer],
            recv_sem=part_recv.at[turn, piece, col],
            device_id=(row, peer),
            device_id_type=MESH,
        )

    def part_arrival(turn, piece, peer):
        return pltpu.make_async_remote_copy(
            src_ref=psend.at[turn, piece, peer],
            dst_ref=precv.at[turn, piece, peer],
            send_sem=part_send.at[turn, piece, peer],
            recv_sem=part_recv.at[turn, piece, peer],
            device_id=(row, peer),
            device_id_type=MESH,
        )

    def columns(piece):
        return slice(piece * width, (piece + 1) * width)

    def apply_inverse(inverse, remain):
        return jnp.dot(inverse, remain, preferred_element_type=jnp.float32)

    def start_gather(turn, piece, level, solved):
        land[turn, piece, row] = pack(solved).astype(jnp.bfloat16)
        for peer in friends:
            gather_copy(turn, piece, peer).start()
        cache[piece, level * n_row + row] = solved.astype(jnp.bfloat16)

    def finish_gather(turn, piece, level):
        for peer in far:
            gather_arrival(turn, piece, peer).wait_recv()
            relay_copy(turn, piece, peer).start()
            cache[piece, level * n_row + peer] = unpack(land[turn, piece, peer], width)
        for slot in [sibling] + near + cross + relayed:
            gather_arrival(turn, piece, slot).wait_recv()
            cache[piece, level * n_row + slot] = unpack(land[turn, piece, slot], width)

    def finish_gather_sends(turn, piece):
        for peer in friends:
            gather_copy(turn, piece, peer).wait_send()
        for peer in far:
            relay_copy(turn, piece, peer).wait_send()

    def row_sum(turn, piece, index, level, peer):
        left = jnp.concatenate([blk[turn, peer, k] for k in range(nnz)], axis=1)
        right = jnp.concatenate(
            [cache[piece, index[level, peer, k]] for k in range(nnz)], axis=0
        )
        return jnp.dot(left, right, preferred_element_type=jnp.float32)

    def send_parts(turn, piece, index, level):
        for peer in ends:
            psend[turn, piece, peer] = pack(row_sum(turn, piece, index, level, peer)).astype(jnp.bfloat16)
            part_copy(turn, piece, peer).start()
        own[piece] = pack(row_sum(turn, piece, index, level, col))

    def take_parts(turn, piece):
        total = own[piece]
        for peer in ends[::-1]:
            part_arrival(turn, piece, peer).wait_recv()
            total = total + precv[turn, piece, peer].astype(jnp.float32)
        return unpack(total, width)

    def finish_part_sends(turn, piece):
        for peer in ends:
            part_copy(turn, piece, peer).wait_send()

    def step(turn, forward, last):
        before = turn if forward else turns - turn
        height = turn + 1 if forward else turns - 1 - turn
        index, level = (lidx, turn) if forward else (uidx, height)
        pltpu.make_async_copy(lblk.at[0], blk.at[turn], blk_sem.at[turn]).wait()
        for piece in range(PIECES):
            finish_gather(turn, piece, before)
            send_parts(turn, piece, index, level)
        for piece in range(PIECES):
            finish_gather_sends(turn, piece)
            source = rhs[height, 0, :, columns(piece)] if forward else fsol[height, piece]
            source = source.astype(jnp.float32)
            remain = (source - take_parts(turn, piece)).astype(jnp.bfloat16)
            solved = apply_inverse(linv[height, 0] if forward else uinv[height, 0], remain)
            if forward and last:
                solved = apply_inverse(uinv[height, 0], solved.astype(jnp.bfloat16))
            if forward or not last:
                start_gather(turn + 1, piece, height, solved)
            if last or not forward:
                out[height, 0, :, columns(piece)] = solved.astype(jnp.bfloat16)
            else:
                fsol[height, piece] = solved.astype(jnp.bfloat16)
            finish_part_sends(turn, piece)
        if last or not forward:
            out_copy(height).start()

    first = []
    for copy in smalls:
        copy.wait()
    for piece in range(PIECES):
        solved = apply_inverse(linv[0, 0], rhs[0, 0, :, columns(piece)])
        fsol[0, piece] = solved.astype(jnp.bfloat16)
        first.append(solved)
    pl.semaphore_wait(barrier, len(friends) + len(ends))
    for piece in range(PIECES):
        start_gather(0, piece, 0, first[piece])

    lax.fori_loop(0, climbs - 1, lambda turn, _: step(turn, True, False), None)
    step(climbs - 1, True, True)
    lax.fori_loop(climbs, turns - 1, lambda turn, _: step(turn, False, False), None)
    step(turns - 1, False, True)
    for height in range(levels):
        out_copy(height).wait()


def shards(
    right_side, lower_inverse, upper_inverse, lower_blocks, lower_index, upper_blocks, upper_index
):
    n_row, n_col = lax.axis_size("prow"), lax.axis_size("pcol")
    levels, _, breadth, columns = right_side.shape
    climbs, rows, nnz = lower_index.shape
    turns = 2 * climbs
    width = columns // PIECES
    packed = (breadth * width // 128, 128)
    bf16 = jnp.bfloat16
    smem = pl.BlockSpec(memory_space=pltpu.SMEM)
    hbm = pl.BlockSpec(memory_space=pl.ANY)
    dma = pltpu.SemaphoreType.DMA
    return pl.pallas_call(
        functools.partial(kernel, n_row, n_col, levels, nnz),
        out_shape=jax.ShapeDtypeStruct(right_side.shape, bf16),
        in_specs=[hbm, hbm, hbm, hbm, hbm, smem, smem],
        out_specs=hbm,
        scratch_shapes=[
            pltpu.VMEM(right_side.shape, bf16),
            pltpu.VMEM(lower_inverse.shape, bf16),
            pltpu.VMEM(upper_inverse.shape, bf16),
            pltpu.VMEM(right_side.shape, bf16),
            pltpu.VMEM((turns, rows, nnz, breadth, breadth), bf16),
            pltpu.VMEM((turns, PIECES, n_row) + packed, bf16),
            pltpu.VMEM((PIECES, levels * n_row, breadth, width), bf16),
            pltpu.VMEM((turns, PIECES, n_col) + packed, bf16),
            pltpu.VMEM((turns, PIECES, n_col) + packed, bf16),
            pltpu.VMEM((PIECES,) + packed, jnp.float32),
            pltpu.VMEM((levels, PIECES, breadth, width), bf16),
            dma((3,)),
            dma((levels,)),
            dma((turns,)),
            dma((turns, PIECES, n_row)),
            dma((turns, PIECES, n_row)),
            dma((turns, PIECES, n_row // 2)),
            dma((turns, PIECES, n_col)),
            dma((turns, PIECES, n_col)),
        ],
        compiler_params=pltpu.CompilerParams(
            collective_id=0, has_side_effects=True, vmem_limit_bytes=62 * 1024 * 1024
        ),
        cost_estimate=pl.CostEstimate(
            flops=2 * turns * rows * nnz * breadth * breadth * columns,
            bytes_accessed=2 * turns * rows * nnz * breadth * breadth,
            transcendentals=0,
        ),
    )(
        right_side, lower_inverse, upper_inverse,
        lower_blocks, upper_blocks, lower_index, upper_index,
    )


def solution(mesh):
    placed = (
        P(None, ("prow", "pcol"), None, None),
        P(None, ("prow", "pcol"), None, None),
        P(None, ("prow", "pcol"), None, None),
        P(None, "prow", "pcol", None, None),
        P(None, "prow", "pcol"),
        P(None, "prow", "pcol", None, None),
        P(None, "prow", "pcol"),
    )
    return jax.shard_map(
        shards,
        mesh=mesh,
        in_specs=placed,
        out_specs=P(None, ("prow", "pcol"), None, None),
        check_vma=False,
    )
```

```python
import functools

import jax
import jax.numpy as jnp
from jax import lax
from jax.experimental import pallas as pl
from jax.experimental.pallas import tpu as pltpu
from jax.sharding import PartitionSpec as P

MESH = pl.DeviceIdType.MESH
PIECES = 2


def flip(index, bits):
    bit = 1
    while bit <= bits:
        if bits & bit:
            index = index + bit - 2 * bit * lax.rem(lax.div(index, bit), 2)
        bit *= 2
    return index


def kernel(
    n_row, n_col, levels, nnz,
    rhs_hbm, linv_hbm, uinv_hbm, lblk, ublk, lidx, uidx, out_hbm,
    rhs, linv, uinv, out, blk, land, cache, psend, precv, own, fsol,
    small_sem, out_sem, blk_sem, gather_send, gather_recv, far_recv, relay_send, part_send, part_recv,
):
    climbs = levels - 1
    turns = 2 * climbs
    width = land.shape[-1]
    row = lax.axis_index("prow")
    col = lax.axis_index("pcol")
    core = lax.rem(row, 2)
    sibling = flip(row, 1)
    strides = range(n_row // 2 - 1, 0, -1)
    far = [flip(row, 2 * j) for j in strides if j & (j - 1)]
    near = [flip(row, 2 * j) for j in strides if not j & (j - 1)]
    cross = [flip(row, 2 * j + 1) for j in strides if not j & (j - 1)]
    relayed = [flip(peer, 1) for peer in far]
    friends = far + [sibling] + near + cross
    ends = [flip(col, j) for j in range(1, n_col)]

    def block_copy(turn):
        source = lblk.at[turn] if turn < climbs else ublk.at[turns - 1 - turn]
        return pltpu.make_async_copy(source, blk.at[turn], blk_sem.at[turn])

    smalls = [
        pltpu.make_async_copy(source, target, small_sem.at[place])
        for place, (source, target) in enumerate(((linv_hbm, linv), (rhs_hbm, rhs), (uinv_hbm, uinv)))
    ]

    def out_copy(height):
        return pltpu.make_async_copy(out.at[height], out_hbm.at[height], out_sem.at[height])

    barrier = pltpu.get_barrier_semaphore()
    for peer in friends:
        pl.semaphore_signal(barrier, inc=1, device_id=(peer, col), device_id_type=MESH)
    for peer in ends:
        pl.semaphore_signal(barrier, inc=1, device_id=(row, peer), device_id_type=MESH)

    for copy in smalls:
        copy.start()
    for turn in range(turns):
        block_copy(turn).start()

    def remote(source, target, send_sem, recv_sem, device):
        return pltpu.make_async_remote_copy(
            src_ref=source, dst_ref=target, send_sem=send_sem, recv_sem=recv_sem,
            device_id=device, device_id_type=MESH,
        )

    def arrival(target, sem):
        return remote(target, target, sem, sem, (sibling, col))

    def relay_copy(turn, piece, peer):
        slot = land.at[turn, piece, peer]
        return remote(
            slot, slot, relay_send.at[turn, piece], gather_recv.at[turn, piece], (sibling, col)
        )

    def part_copy(turn, piece, j):
        return remote(
            psend.at[turn, piece, j], precv.at[turn, piece, j],
            part_send.at[turn, piece], part_recv.at[turn, piece], (row, ends[j]),
        )

    def columns(piece):
        return pl.ds(pl.multiple_of(piece * width, width), width)

    def apply_inverse(inverse, remain):
        return jnp.dot(inverse, remain, preferred_element_type=jnp.float32).astype(jnp.bfloat16)

    def start_gather(turn, piece):
        slot = land.at[turn, piece, row]
        for i, peer in enumerate(far):
            remote(
                slot, slot, gather_send.at[turn, piece], far_recv.at[turn, piece, i], (peer, col)
            ).start()
        for peer in friends[len(far):]:
            remote(
                slot, slot, gather_send.at[turn, piece], gather_recv.at[turn, piece], (peer, col)
            ).start()

    def finish_gather(turn, piece, level):
        for i, peer in enumerate(far):
            arrival(land.at[turn, piece, peer], far_recv.at[turn, piece, i]).wait_recv()
            relay_copy(turn, piece, peer).start()
        rest = n_row - 1 - len(far)
        arrival(land.at[turn, piece, pl.ds(0, rest)], gather_recv.at[turn, piece]).wait_recv()
        cache[piece, pl.ds(level * n_row, n_row)] = land[turn, piece]

    def finish_gather_sends(turn, piece):
        sent = land.at[turn, piece, pl.ds(0, len(friends))]
        arrival(sent, gather_send.at[turn, piece]).wait_send()
        if far:
            sent = land.at[turn, piece, pl.ds(0, len(far))]
            arrival(sent, relay_send.at[turn, piece]).wait_send()

    def row_sum(turn, piece, index, level, peer):
        left = jnp.concatenate([blk[turn, peer, k] for k in range(nnz)], axis=1)
        right = jnp.concatenate(
            [cache[piece, index[level, peer, k]] for k in range(nnz)], axis=0
        )
        return jnp.dot(left, right, preferred_element_type=jnp.float32)

    def send_parts(turn, piece, index, level):
        for j in range(len(ends) - 1, -1, -1):
            value = row_sum(turn, piece, index, level, ends[j])
            psend[turn, piece, j] = value.astype(jnp.bfloat16)
            part_copy(turn, piece, j).start()
        own[piece] = row_sum(turn, piece, index, level, col)

    def take_parts(turn, piece):
        arrival(precv.at[turn, piece], part_recv.at[turn, piece]).wait_recv()
        total = own[piece]
        for j in range(len(ends)):
            total = total + precv[turn, piece, j].astype(jnp.float32)
        return total

    def step(turn, forward):
        before = turn if forward else turns - turn
        height = turn + 1 if forward else turns - 1 - turn
        index, level = (lidx, turn) if forward else (uidx, height)
        pltpu.make_async_copy(lblk.at[0], blk.at[turn], blk_sem.at[turn]).wait()

        def spread(piece, _):
            finish_gather(turn, piece, before)
            send_parts(turn, piece, index, level)

        def settle(piece, _):
            finish_gather_sends(turn, piece)
            source = rhs[height, 0, :, columns(piece)] if forward else fsol[height, piece]
            total = take_parts(turn, piece)
            remain = (source.astype(jnp.float32) - total).astype(jnp.bfloat16)
            if forward:
                solved = apply_inverse(linv[height, 0], remain)

                @pl.when(turn < climbs - 1)
                def _():
                    land[turn + 1, piece, row] = solved
                    fsol[height, piece] = solved

                @pl.when(turn == climbs - 1)
                def _():
                    top = apply_inverse(uinv[height, 0], solved)
                    land[turn + 1, piece, row] = top
                    out[height, 0, :, columns(piece)] = top

                start_gather(turn + 1, piece)
            else:
                solved = apply_inverse(uinv[height, 0], remain)

                @pl.when(turn < turns - 1)
                def _():
                    land[turn + 1, piece, row] = solved
                    start_gather(turn + 1, piece)

                out[height, 0, :, columns(piece)] = solved
            arrival(psend.at[turn, piece], part_send.at[turn, piece]).wait_send()

        lax.fori_loop(0, PIECES, spread, None)
        lax.fori_loop(0, PIECES, settle, None)
        if forward:
            @pl.when(turn == climbs - 1)
            def _():
                out_copy(height).start()
        else:
            out_copy(height).start()

    for copy in smalls:
        copy.wait()

    def begin(piece, _):
        solved = apply_inverse(linv[0, 0], rhs[0, 0, :, columns(piece)])
        land[0, piece, row] = solved
        fsol[0, piece] = solved

    lax.fori_loop(0, PIECES, begin, None)
    pl.semaphore_wait(barrier, len(friends) + len(ends))
    for piece in range(PIECES):
        start_gather(0, piece)

    lax.fori_loop(0, climbs, lambda turn, _: step(turn, True), None)
    lax.fori_loop(climbs, turns, lambda turn, _: step(turn, False), None)
    for height in range(levels):
        out_copy(height).wait()


def shards(
    right_side, lower_inverse, upper_inverse, lower_blocks, lower_index, upper_blocks, upper_index
):
    n_row, n_col = lax.axis_size("prow"), lax.axis_size("pcol")
    levels, _, breadth, columns = right_side.shape
    climbs, rows, nnz = lower_index.shape
    turns = 2 * climbs
    width = columns // PIECES
    bf16 = jnp.bfloat16
    smem = pl.BlockSpec(memory_space=pltpu.SMEM)
    hbm = pl.BlockSpec(memory_space=pl.ANY)
    dma = pltpu.SemaphoreType.DMA
    return pl.pallas_call(
        functools.partial(kernel, n_row, n_col, levels, nnz),
        out_shape=jax.ShapeDtypeStruct(right_side.shape, bf16),
        in_specs=[hbm, hbm, hbm, hbm, hbm, smem, smem],
        out_specs=hbm,
        scratch_shapes=[
            pltpu.VMEM(right_side.shape, bf16),
            pltpu.VMEM(lower_inverse.shape, bf16),
            pltpu.VMEM(upper_inverse.shape, bf16),
            pltpu.VMEM(right_side.shape, bf16),
            pltpu.VMEM((turns, rows, nnz, breadth, breadth), bf16),
            pltpu.VMEM((turns, PIECES, n_row, breadth, width), bf16),
            pltpu.VMEM((PIECES, levels * n_row, breadth, width), bf16),
            pltpu.VMEM((turns, PIECES, n_col - 1, breadth, width), bf16),
            pltpu.VMEM((turns, PIECES, n_col - 1, breadth, width), bf16),
            pltpu.VMEM((PIECES, breadth, width), jnp.float32),
            pltpu.VMEM((levels, PIECES, breadth, width), bf16),
            dma((3,)),
            dma((levels,)),
            dma((turns,)),
            dma((turns, PIECES)),
            dma((turns, PIECES)),
            dma((turns, PIECES, max(1, n_row // 2))),
            dma((turns, PIECES)),
            dma((turns, PIECES)),
            dma((turns, PIECES)),
        ],
        compiler_params=pltpu.CompilerParams(
            collective_id=0, has_side_effects=True, vmem_limit_bytes=58 * 1024 * 1024
        ),
        cost_estimate=pl.CostEstimate(
            flops=2 * turns * rows * nnz * breadth * breadth * columns,
            bytes_accessed=2 * turns * rows * nnz * breadth * breadth,
            transcendentals=0,
        ),
    )(
        right_side, lower_inverse, upper_inverse,
        lower_blocks, upper_blocks, lower_index, upper_index,
    )


def solution(mesh):
    placed = (
        P(None, ("prow", "pcol"), None, None),
        P(None, ("prow", "pcol"), None, None),
        P(None, ("prow", "pcol"), None, None),
        P(None, "prow", "pcol", None, None),
        P(None, "prow", "pcol"),
        P(None, "prow", "pcol", None, None),
        P(None, "prow", "pcol"),
    )
    return jax.shard_map(
        shards,
        mesh=mesh,
        in_specs=placed,
        out_specs=P(None, ("prow", "pcol"), None, None),
        check_vma=False,
    )
```
